32 devices in a mesh: ctx: 8 (over z, x), fsdp: 4 (over y, core).
Axes of the slice: x: 2, y: 2, z: 4, core: 2. Of those that a mesh axis runs over, the one named last changes fastest.
Arguments:
- hidden_in: bfloat16 [4, 1024, 1536], P('fsdp', 'ctx'), may hold values from -6 to 6
- cotangent: bfloat16 [4, 1024, 1536], P('fsdp', 'ctx'), may hold values from -6 to 6
- block_order: int32 [4, 16], P('fsdp'), may hold values from 0 to 15, as said below
- rotary_positions: int32 [4, 1024], P('fsdp', 'ctx'), may hold values from 0 to 2046, as said below
- attn_gain: bfloat16 [1536], P(('ctx', 'fsdp')), may hold values from 0.25 to 1.75
- qk_gain: bfloat16 [128], P(('ctx', 'fsdp')), may hold values from 0.25 to 1.75
- w_query: bfloat16 [1536, 1536], P(('ctx', 'fsdp')), may hold values from -0.15625 to 0.15625
- key_projection: bfloat16 [1536, 512], P(('ctx', 'fsdp')), may hold values from -0.15625 to 0.15625
- value_projection: bfloat16 [1536, 512], P(('ctx', 'fsdp')), may hold values from -0.15625 to 0.15625
- w_output: bfloat16 [1536, 1536], P(('ctx', 'fsdp')), may hold values from -1 to 1
- ffn_gain: bfloat16 [1536], P(('ctx', 'fsdp')), may hold values from 0.25 to 1.75
- w_gate: bfloat16 [1536, 4608], P(('ctx', 'fsdp')), may hold values from -0.15625 to 0.15625
- w_up: bfloat16 [1536, 4608], P(('ctx', 'fsdp')), may hold values from -0.15625 to 0.15625
- w_down: bfloat16 [4608, 1536], P(('ctx', 'fsdp')), may hold values from -0.09375 to 0.09375
Outputs:
- block_out: bfloat16 [4, 1024, 1536], P('fsdp', 'ctx')
- grad_in: bfloat16 [4, 1024, 1536], P('fsdp', 'ctx')
- grad_attn_gain: float32 [1536], P(('ctx', 'fsdp'))
- grad_qk_gain: float32 [128], P(('ctx', 'fsdp'))
- grad_w_query: float32 [1536, 1536], P(('ctx', 'fsdp'))
- grad_w_key: float32 [1536, 512], P(('ctx', 'fsdp'))
- grad_w_value: float32 [1536, 512], P(('ctx', 'fsdp'))
- grad_w_output: float32 [1536, 1536], P(('ctx', 'fsdp'))
- grad_ffn_gain: float32 [1536], P(('ctx', 'fsdp'))
- grad_w_gate: float32 [1536, 4608], P(('ctx', 'fsdp'))
- grad_w_up: float32 [1536, 4608], P(('ctx', 'fsdp'))
- grad_w_down: float32 [4608, 1536], P(('ctx', 'fsdp'))
The draws below stay inside these ranges and needn't reach their ends.
Inputs may be any that keep to these rules, and one draw needn't show every extreme that they name: Row s is an ordering of the 16 blocks of 64 consecutive tokens of sequence s: stored slot j holds block block_order[s, j], so device i of ctx holds slots 2 i and 2 i + 1. `rotary_positions`: A token's rotary position is its place in its sequence (seq_index) plus one start per sequence, the start from 0 to 1023; the first sequence starts at 0 and the last at 1023.
All inputs are finite; a program needn't handle non-finite values.
Results may differ from the reference program's by a relative error of at most 0.019.
Values may be sent and summed in bfloat16 or wider, within the bound.
A program may use at most 384 MiB of HBM per device.

```python
import math
import jax
import jax.numpy as jnp
from jax import lax

MODEL_WIDTH = 1536
QUERY_HEADS = 24
KEY_VALUE_HEADS = 8
HEAD_SIZE = 64
FF = 4608
SEQS = 4
SEQUENCE_LENGTH = 1024
BLOCKS = 16
BLOCK = 64


def shared_order(key):
    key_rows = jax.random.split(key, SEQS)
    return jax.vmap(lambda single: jax.random.permutation(single, BLOCKS))(key_rows).astype(jnp.int32)


def draw_block_order(key, part):
    order = shared_order(key)
    return order


def draw_rotary_positions(key, part):
    order = shared_order(key)
    key = jax.random.fold_in(key, 23)
    starts = jax.random.randint(key, (SEQS, 1), 0, SEQUENCE_LENGTH).astype(jnp.int32)
    starts = starts.at[0, 0].set(0).at[SEQS - 1, 0].set(SEQUENCE_LENGTH - 1)
    offsets = jnp.arange(BLOCK, dtype=jnp.int32)
    index = (order[:, :, None] * BLOCK + offsets[None, None, :]).reshape(SEQS, SEQUENCE_LENGTH)
    return (index + starts).astype(jnp.int32)


def block_levels(rng, extent, cuts, smallest, top_value):
    loudness, own = 1.0, jax.random.fold_in(rng, 6)
    for axis_at, blocks in cuts:
        steps = jnp.exp(jax.random.uniform(jax.random.fold_in(own, axis_at), (blocks,), jnp.float32, smallest / len(cuts), top_value / len(cuts)))
        loudness = loudness * jnp.repeat(steps, extent[axis_at] // blocks).reshape([-1 if axis == axis_at else 1 for axis in range(len(extent))])
    return loudness


def normal_values(key, dims, deviation, most, cuts=(), kind=jnp.bfloat16):
    factor_of = block_levels(key, dims, cuts, -0.22, 0.18) if cuts else 1.0
    array = jax.random.normal(key, dims, jnp.float32) * deviation * factor_of
    return jnp.minimum(jnp.maximum(array, -most), most).astype(kind)


def setup_inputs(seed: int = 0) -> dict:
    arg_keys = jax.random.split(jax.random.key(seed), 15)
    return {
        "hidden_in": normal_values(arg_keys[0], (SEQS, SEQUENCE_LENGTH, MODEL_WIDTH), 1.0, 6.0, ((0, 4), (1, 8))),
        "cotangent": normal_values(arg_keys[1], (SEQS, SEQUENCE_LENGTH, MODEL_WIDTH), 1.0, 6.0, ((0, 4), (1, 8))),
        "block_order": draw_block_order(jax.random.fold_in(arg_keys[14], 71), 0),
        "rotary_positions": draw_rotary_positions(jax.random.fold_in(arg_keys[14], 71), 0),
        "attn_gain": jnp.clip(1.0 + 0.15 * jax.random.normal(arg_keys[4], (MODEL_WIDTH,), jnp.float32), 0.25, 1.75).astype(jnp.bfloat16),
        "qk_gain": jnp.clip(1.0 + 0.15 * jax.random.normal(arg_keys[5], (2 * HEAD_SIZE,), jnp.float32), 0.25, 1.75).astype(jnp.bfloat16),
        "w_query": normal_values(arg_keys[6], (MODEL_WIDTH, QUERY_HEADS * HEAD_SIZE), MODEL_WIDTH ** -0.5, 0.15625, ((0, 32),)),
        "key_projection": normal_values(arg_keys[7], (MODEL_WIDTH, KEY_VALUE_HEADS * HEAD_SIZE), MODEL_WIDTH ** -0.5, 0.15625, ((0, 32),)),
        "value_projection": normal_values(arg_keys[8], (MODEL_WIDTH, KEY_VALUE_HEADS * HEAD_SIZE), MODEL_WIDTH ** -0.5, 0.15625, ((0, 32),)),
        "w_output": normal_values(arg_keys[9], (QUERY_HEADS * HEAD_SIZE, MODEL_WIDTH), (HEAD_SIZE // 2) ** -0.5, 1.0, ((0, 32),)),
        "ffn_gain": jnp.clip(1.0 + 0.15 * jax.random.normal(arg_keys[10], (MODEL_WIDTH,), jnp.float32), 0.25, 1.75).astype(jnp.bfloat16),
        "w_gate": normal_values(arg_keys[11], (MODEL_WIDTH, FF), MODEL_WIDTH ** -0.5, 0.15625, ((0, 32),)),
        "w_up": normal_values(arg_keys[12], (MODEL_WIDTH, FF), MODEL_WIDTH ** -0.5, 0.15625, ((0, 32),)),
        "w_down": normal_values(arg_keys[13], (FF, MODEL_WIDTH), FF ** -0.5, 0.09375, ((0, 32),)),
    }


EPS = 1e-05
THETA = 1000000.0
HIGH_PRECISION = lax.Precision.HIGHEST

@jax.custom_vjp
def lower_precision(v):
    return lax.optimization_barrier(v.astype(jnp.bfloat16)).astype(jnp.float32)

@jax.custom_vjp
def lower_precision_backward(v):
    return v

def low_keep(v):
    return (lower_precision(v), None)

def low_pass(kept, grad):
    return (grad,)

def back_keep(v):
    return (v, None)

def back_low(kept, grad):
    return (lower_precision(grad),)
lower_precision.defvjp(low_keep, low_pass)
lower_precision_backward.defvjp(back_keep, back_low)

def rms_scale(value_matrix_rows, gain):
    return value_matrix_rows * lax.rsqrt(lax.optimization_barrier(jnp.mean(value_matrix_rows * value_matrix_rows, axis=-1, keepdims=True)) + EPS) * gain

def frequencies():
    return jnp.exp(-math.log(THETA) * 2.0 * jnp.arange(HEAD_SIZE // 2, dtype=jnp.float32) / HEAD_SIZE)

def apply_rotary(value_matrix_rows, rotary_angles):
    half = HEAD_SIZE // 2
    cosine = jnp.cos(rotary_angles)[:, None, :]
    sine = jnp.sin(rotary_angles)[:, None, :]
    first = value_matrix_rows[..., :half]
    second = value_matrix_rows[..., half:]
    return jnp.concatenate([first * cosine - second * sine, second * cosine + first * sine], axis=-1)

def attend(query_rows, key, value_rows, index):
    queries_per_group = QUERY_HEADS // KEY_VALUE_HEADS
    rows_per_block = math.gcd(SEQUENCE_LENGTH, 256)
    token_count = SEQUENCE_LENGTH // rows_per_block
    grouped_heads = query_rows.reshape(token_count, rows_per_block, KEY_VALUE_HEADS, queries_per_group, HEAD_SIZE)
    rows_index = index.reshape(token_count, rows_per_block)

    def one_block(item):
        part, part_index = item
        scores = jnp.einsum('qhgd,khd->hgqk', part, key, precision=HIGH_PRECISION) / math.sqrt(HEAD_SIZE)
        scores = lower_precision_backward(scores)
        allowed = index[None, :] <= part_index[:, None]
        scores = jnp.where(allowed, scores, -jnp.inf)
        probs = jax.nn.softmax(scores, axis=-1)
        return jnp.einsum('hgqk,khd->qhgd', lower_precision(probs), value_rows, precision=HIGH_PRECISION)
    mixed = lax.map(jax.checkpoint(one_block), (grouped_heads, rows_index))
    return mixed.reshape(SEQUENCE_LENGTH, QUERY_HEADS * HEAD_SIZE)

def layer(weights, hidden, rotary_angles, index):
    attn_gain, qk_gain, w_query, key_projection, value_projection, w_output, ffn_gain, w_gate, w_up, w_down = weights
    normalized_input = lower_precision(rms_scale(hidden, attn_gain))
    query_rows = lower_precision_backward(jnp.dot(normalized_input, w_query, precision=HIGH_PRECISION)).reshape(SEQUENCE_LENGTH, QUERY_HEADS, HEAD_SIZE)
    key = lower_precision_backward(jnp.dot(normalized_input, key_projection, precision=HIGH_PRECISION)).reshape(SEQUENCE_LENGTH, KEY_VALUE_HEADS, HEAD_SIZE)
    value_rows = lower_precision(lower_precision_backward(jnp.dot(normalized_input, value_projection, precision=HIGH_PRECISION))).reshape(SEQUENCE_LENGTH, KEY_VALUE_HEADS, HEAD_SIZE)
    query_rows = lower_precision(apply_rotary(rms_scale(query_rows, qk_gain[:HEAD_SIZE]), rotary_angles))
    key = lower_precision(apply_rotary(rms_scale(key, qk_gain[HEAD_SIZE:]), rotary_angles))
    mixed = lower_precision(lower_precision_backward(attend(query_rows, key, value_rows, index)))
    middle = hidden + lower_precision_backward(jnp.dot(mixed, w_output, precision=HIGH_PRECISION))
    normed_two = lower_precision(rms_scale(middle, ffn_gain))
    gate = lower_precision_backward(jnp.dot(normed_two, w_gate, precision=HIGH_PRECISION))
    up = lower_precision_backward(jnp.dot(normed_two, w_up, precision=HIGH_PRECISION))
    inner = lower_precision(jax.nn.silu(gate) * up)
    return middle + jnp.dot(inner, w_down, precision=HIGH_PRECISION)

def reference(hidden_in, cotangent, block_order, rotary_positions, attn_gain, qk_gain, w_query, key_projection, value_projection, w_output, ffn_gain, w_gate, w_up, w_down):
    params = tuple((weight.astype(jnp.float32) for weight in (attn_gain, qk_gain, w_query, key_projection, value_projection, w_output, ffn_gain, w_gate, w_up, w_down)))
    offsets = jnp.arange(BLOCK, dtype=jnp.int32)

    def one_sequence(total, item):
        hidden, grad_out, order, positions = item
        index = (order[:, None] * BLOCK + offsets[None, :]).reshape(SEQUENCE_LENGTH).astype(jnp.int32)
        rotary_angles = positions.astype(jnp.float32)[:, None] * frequencies()[None, :]

        def forward(weights, value_matrix_rows):
            return layer(weights, value_matrix_rows, rotary_angles, index)
        result, pull = jax.vjp(forward, params, hidden.astype(jnp.float32))
        grads, grad_hidden = pull(grad_out.astype(jnp.float32))
        total = jax.tree.map(jnp.add, total, grads)
        return (total, (result.astype(jnp.bfloat16), grad_hidden.astype(jnp.bfloat16)))
    start = jax.tree.map(jnp.zeros_like, params)
    total, outputs = lax.scan(one_sequence, start, (hidden_in, cotangent, block_order, rotary_positions))
    block_out, grad_in = outputs
    return (block_out, grad_in, total[0], total[1], total[2], total[3], total[4], total[5], total[6], total[7], total[8], total[9])
```

```python
import math

import jax
import jax.numpy as jnp
from jax import lax
from jax.experimental import pallas as pl
from jax.experimental.pallas import tpu as pltpu
from jax.sharding import PartitionSpec as P

QUERY_HEADS = 24
KEY_VALUE_HEADS = 8
HEAD_SIZE = 64


EPS = 1e-05
THETA = 1000000.0


def frequencies(model_width):
    return jnp.exp(
        -math.log(THETA) * 2.0 * jnp.arange(model_width // 2, dtype=jnp.float32) / model_width
    )


def apply_rotary(value_matrix_rows, rotary_angles):
    half = value_matrix_rows.shape[-1] // 2
    cosine = jnp.cos(rotary_angles)[:, None, :]
    sine = jnp.sin(rotary_angles)[:, None, :]
    first = value_matrix_rows[..., :half]
    second = value_matrix_rows[..., half:]
    return jnp.concatenate(
        [first * cosine - second * sine, second * cosine + first * sine], axis=-1
    )


def rotary_backward(grads, rotary_angles):
    half = grads.shape[-1] // 2
    cosine = jnp.cos(rotary_angles)[:, None, :]
    sine = jnp.sin(rotary_angles)[:, None, :]
    first = grads[..., :half]
    second = grads[..., half:]
    return jnp.concatenate(
        [first * cosine + second * sine, second * cosine - first * sine], axis=-1
    )


def norm_backward(value_matrix_rows, inverse, gain, grads):
    weighted = grads * gain
    return inverse * weighted - inverse * inverse * inverse * value_matrix_rows * jnp.mean(
        weighted * value_matrix_rows, axis=-1, keepdims=True
    )


def lookup(table, slots):
    matches = slots[:, None] == jnp.arange(table.shape[0], dtype=jnp.int32)[None, :]
    return jnp.sum(jnp.where(matches, table[None, :], 0), axis=1)


def sequence_index(table, places, half_rows):
    return lookup(table, places // half_rows) * half_rows + places % half_rows


def block_scores(grouped_heads, key_rows):
    model_width = key_rows.shape[0]
    reshaped_heads = key_rows.reshape(model_width, KEY_VALUE_HEADS, HEAD_SIZE)
    return jnp.einsum(
        "thgd,khd->hgtk", grouped_heads, reshaped_heads, preferred_element_type=jnp.float32
    ) * (1.0 / math.sqrt(HEAD_SIZE))


def owner_totals(received):
    return tuple((jnp.sum(piece, axis=0) for piece in received))


def sweep(state, pieces, start, step, table, half_rows, last_query):
    token_count = pieces[0].shape[0]
    model_width = max(
        (size for size in range(1, min(token_count, 512) + 1) if token_count % size == 0)
    )
    turns = token_count // model_width
    stacked = tuple((piece.reshape((turns, model_width) + piece.shape[1:]) for piece in pieces))
    offsets = start + model_width * jnp.arange(turns, dtype=jnp.int32)

    def visit(carry, item):
        parts, position_shift = item
        key_index = sequence_index(
            table, position_shift + jnp.arange(model_width, dtype=jnp.int32), half_rows
        )
        live = jnp.min(key_index) <= last_query
        carry = lax.cond(
            live,
            lambda inner: step(inner, parts, position_shift, key_index),
            lambda inner: inner,
            carry,
        )
        return (carry, None)

    state, unused = lax.scan(visit, state, (stacked, offsets))
    return state


def general_plan(
    hidden_in,
    cotangent,
    block_order,
    rotary_positions,
    attn_gain,
    qk_gain,
    w_query,
    key_projection,
    value_projection,
    w_output,
    ffn_gain,
    w_gate,
    w_up,
    w_down,
):
    single_float = jnp.float32
    brain_float_half = jnp.bfloat16
    gathered = (
        lax.all_gather(attn_gain, ("ctx", "fsdp"), axis=0, tiled=True),
        lax.all_gather(qk_gain, ("ctx", "fsdp"), axis=0, tiled=True),
        lax.all_gather(w_query, ("ctx", "fsdp"), axis=0, tiled=True),
        lax.all_gather(key_projection, ("ctx", "fsdp"), axis=0, tiled=True),
        lax.all_gather(value_projection, ("ctx", "fsdp"), axis=0, tiled=True),
        lax.all_gather(w_output, ("ctx", "fsdp"), axis=0, tiled=True),
        lax.all_gather(ffn_gain, ("ctx", "fsdp"), axis=0, tiled=True),
        lax.all_gather(w_gate, ("ctx", "fsdp"), axis=0, tiled=True),
        lax.all_gather(w_up, ("ctx", "fsdp"), axis=0, tiled=True),
        lax.all_gather(w_down, ("ctx", "fsdp"), axis=0, tiled=True),
    )
    gain_one, gain_both, query_w, key_matrix, value_w, output_w, gain_two, gate_w, up_w, down_w = (
        gathered
    )
    gain_one = gain_one.astype(single_float)
    gain_two = gain_two.astype(single_float)
    gain_query = gain_both[:HEAD_SIZE].astype(single_float)
    key_norm_gain = gain_both[HEAD_SIZE:].astype(single_float)
    queries_per_group = QUERY_HEADS // KEY_VALUE_HEADS
    hidden = hidden_in[0].astype(single_float)
    grad_out = cotangent[0]
    token_rows = hidden.shape[0]
    half_rows = token_rows // 2
    sequence_span = token_rows * lax.axis_size("ctx")
    order = block_order[0]
    place = lax.axis_index("ctx")
    local_rows = jnp.arange(token_rows, dtype=jnp.int32)
    my_index = sequence_index(order, place * token_rows + local_rows, half_rows)
    last_query = jnp.max(my_index)
    rotary_angles = (
        rotary_positions[0].astype(single_float)[:, None] * frequencies(HEAD_SIZE)[None, :]
    )
    inv_one = lax.rsqrt(jnp.mean(hidden * hidden, axis=-1, keepdims=True) + EPS)
    normalized_input = (hidden * inv_one * gain_one).astype(brain_float_half)
    query_rows = jnp.dot(normalized_input, query_w, preferred_element_type=single_float).reshape(
        token_rows, QUERY_HEADS, HEAD_SIZE
    )
    key = jnp.dot(normalized_input, key_matrix, preferred_element_type=single_float).reshape(
        token_rows, KEY_VALUE_HEADS, HEAD_SIZE
    )
    value_rows = jnp.dot(normalized_input, value_w, preferred_element_type=single_float).astype(
        brain_float_half
    )
    inv_query = lax.rsqrt(jnp.mean(query_rows * query_rows, axis=-1, keepdims=True) + EPS)
    key_inverse_norm = lax.rsqrt(jnp.mean(key * key, axis=-1, keepdims=True) + EPS)
    rotated_query = apply_rotary(query_rows * inv_query * gain_query, rotary_angles).astype(
        brain_float_half
    )
    rotated_key = (
        apply_rotary(key * key_inverse_norm * key_norm_gain, rotary_angles)
        .astype(brain_float_half)
        .reshape(token_rows, KEY_VALUE_HEADS * HEAD_SIZE)
    )
    grouped_heads = rotated_query.reshape(token_rows, KEY_VALUE_HEADS, queries_per_group, HEAD_SIZE)

    def allowed_of(key_index):
        return (key_index[None, :] <= my_index[:, None])[None, None]

    def stats_step(carry, parts, position_shift, key_index):
        running, total = carry
        scores = jnp.where(allowed_of(key_index), block_scores(grouped_heads, parts[0]), -jnp.inf)
        newer = jnp.maximum(running, jnp.max(scores, axis=-1))
        total = total * jnp.exp(running - newer) + jnp.sum(
            jnp.exp(scores - newer[..., None]), axis=-1
        )
        return (newer, total)

    statistic_shape = (KEY_VALUE_HEADS, queries_per_group, token_rows)
    running, total = sweep(
        (jnp.full(statistic_shape, -1e30, single_float), jnp.zeros(statistic_shape, single_float)),
        (lax.all_gather(rotated_key, "ctx", axis=0, tiled=True),),
        jnp.int32(0),
        stats_step,
        order,
        half_rows,
        last_query,
    )
    log_total = running + jnp.log(total)

    def probs_of(key_rows, key_index):
        return jnp.where(
            allowed_of(key_index),
            jnp.exp(block_scores(grouped_heads, key_rows) - log_total[..., None]),
            0.0,
        )

    def mix_step(carry, parts, position_shift, key_index):
        key_rows, value_matrix_rows = parts
        probs_low = probs_of(key_rows, key_index).astype(brain_float_half)
        reshaped_heads = value_matrix_rows.reshape(key_rows.shape[0], KEY_VALUE_HEADS, HEAD_SIZE)
        return carry + jnp.einsum(
            "hgtk,khd->thgd", probs_low, reshaped_heads, preferred_element_type=single_float
        )

    mixed_sum = sweep(
        jnp.zeros((token_rows, KEY_VALUE_HEADS, queries_per_group, HEAD_SIZE), single_float),
        (
            lax.all_gather(rotated_key, "ctx", axis=0, tiled=True),
            lax.all_gather(value_rows, "ctx", axis=0, tiled=True),
        ),
        jnp.int32(0),
        mix_step,
        order,
        half_rows,
        last_query,
    )
    mixed = mixed_sum.reshape(token_rows, QUERY_HEADS * HEAD_SIZE).astype(brain_float_half)
    middle = hidden + jnp.dot(mixed, output_w, preferred_element_type=single_float)
    inv_two = lax.rsqrt(jnp.mean(middle * middle, axis=-1, keepdims=True) + EPS)
    normed_two = (middle * inv_two * gain_two).astype(brain_float_half)
    gate = jnp.dot(normed_two, gate_w, preferred_element_type=single_float)
    up = jnp.dot(normed_two, up_w, preferred_element_type=single_float)
    sigmoid_gate = jax.nn.sigmoid(gate)
    active = gate * sigmoid_gate
    inner = (active * up).astype(brain_float_half)
    block_out = (middle + jnp.dot(inner, down_w, preferred_element_type=single_float)).astype(
        brain_float_half
    )
    regathered = (
        lax.all_gather(attn_gain, ("ctx", "fsdp"), axis=0, tiled=True),
        lax.all_gather(qk_gain, ("ctx", "fsdp"), axis=0, tiled=True),
        lax.all_gather(w_query, ("ctx", "fsdp"), axis=0, tiled=True),
        lax.all_gather(key_projection, ("ctx", "fsdp"), axis=0, tiled=True),
        lax.all_gather(value_projection, ("ctx", "fsdp"), axis=0, tiled=True),
        lax.all_gather(w_output, ("ctx", "fsdp"), axis=0, tiled=True),
        lax.all_gather(ffn_gain, ("ctx", "fsdp"), axis=0, tiled=True),
        lax.all_gather(w_gate, ("ctx", "fsdp"), axis=0, tiled=True),
        lax.all_gather(w_up, ("ctx", "fsdp"), axis=0, tiled=True),
        lax.all_gather(w_down, ("ctx", "fsdp"), axis=0, tiled=True),
    )
    (
        unused_one,
        unused_both,
        query_w,
        key_matrix,
        value_w,
        output_w,
        unused_two,
        gate_w,
        up_w,
        down_w,
    ) = regathered
    grad_w_down = jnp.einsum("tf,td->fd", inner, grad_out, preferred_element_type=single_float)
    grad_inner = jnp.einsum("td,fd->tf", grad_out, down_w, preferred_element_type=single_float)
    grad_gate = (grad_inner * up * sigmoid_gate * (1.0 + gate * (1.0 - sigmoid_gate))).astype(
        brain_float_half
    )
    grad_up = (grad_inner * active).astype(brain_float_half)
    grad_w_gate = jnp.einsum(
        "td,tf->df", normed_two, grad_gate, preferred_element_type=single_float
    )
    grad_w_up = jnp.einsum("td,tf->df", normed_two, grad_up, preferred_element_type=single_float)
    grad_normed_two = jnp.einsum(
        "tf,df->td", grad_gate, gate_w, preferred_element_type=single_float
    ) + jnp.einsum("tf,df->td", grad_up, up_w, preferred_element_type=single_float)
    grad_ffn_gain = jnp.sum(grad_normed_two * middle * inv_two, axis=0)
    grad_middle = grad_out.astype(single_float) + norm_backward(
        middle, inv_two, gain_two, grad_normed_two
    )
    grad_branch = grad_middle.astype(brain_float_half)
    grad_w_output = jnp.einsum("tq,td->qd", mixed, grad_branch, preferred_element_type=single_float)
    mixed_gradient = jnp.einsum(
        "td,qd->tq", grad_branch, output_w, preferred_element_type=single_float
    ).astype(brain_float_half)
    gradient_of_grouped = mixed_gradient.reshape(
        token_rows, KEY_VALUE_HEADS, queries_per_group, HEAD_SIZE
    )
    delta = jnp.transpose(
        jnp.sum(gradient_of_grouped.astype(single_float) * mixed_sum, axis=-1), (1, 2, 0)
    )

    def back_step(carry, parts, position_shift, key_index):
        grad_query_acc, key_gradient_total, value_gradient_total = carry
        key_rows, value_matrix_rows = parts
        model_width = key_rows.shape[0]
        probs = probs_of(key_rows, key_index)
        probs_low = probs.astype(brain_float_half)
        reshaped_keys = key_rows.reshape(model_width, KEY_VALUE_HEADS, HEAD_SIZE)
        reshaped_values = value_matrix_rows.reshape(model_width, KEY_VALUE_HEADS, HEAD_SIZE)
        grad_probs = jnp.einsum(
            "thgd,khd->hgtk",
            gradient_of_grouped,
            reshaped_values,
            preferred_element_type=single_float,
        )
        grad_scores = (probs * (grad_probs - delta[..., None])).astype(brain_float_half)
        grad_query_acc = grad_query_acc + jnp.einsum(
            "hgtk,khd->thgd", grad_scores, reshaped_keys, preferred_element_type=single_float
        )
        keys_gradient = jnp.einsum(
            "hgtk,thgd->khd", grad_scores, grouped_heads, preferred_element_type=single_float
        ) * (1.0 / math.sqrt(HEAD_SIZE))
        values_gradient = jnp.einsum(
            "hgtk,thgd->khd", probs_low, gradient_of_grouped, preferred_element_type=single_float
        )
        key_gradient_total = lax.dynamic_update_slice_in_dim(
            key_gradient_total,
            keys_gradient.reshape(model_width, KEY_VALUE_HEADS * HEAD_SIZE),
            position_shift,
            0,
        )
        value_gradient_total = lax.dynamic_update_slice_in_dim(
            value_gradient_total,
            values_gradient.reshape(model_width, KEY_VALUE_HEADS * HEAD_SIZE),
            position_shift,
            0,
        )
        return (grad_query_acc, key_gradient_total, value_gradient_total)

    zero_gradients = jnp.zeros((sequence_span, KEY_VALUE_HEADS * HEAD_SIZE), single_float)
    grad_query_acc, key_gradient_total, value_gradient_total = sweep(
        (
            jnp.zeros((token_rows, KEY_VALUE_HEADS, queries_per_group, HEAD_SIZE), single_float),
            zero_gradients,
            zero_gradients,
        ),
        (
            lax.all_gather(rotated_key, "ctx", axis=0, tiled=True),
            lax.all_gather(value_rows, "ctx", axis=0, tiled=True),
        ),
        jnp.int32(0),
        back_step,
        order,
        half_rows,
        last_query,
    )
    key_gradient_local, grad_value_own = (
        lax.psum_scatter(
            key_gradient_total.astype(jnp.bfloat16), "ctx", scatter_dimension=0, tiled=True
        ).astype(jnp.float32),
        lax.psum_scatter(
            value_gradient_total.astype(jnp.bfloat16), "ctx", scatter_dimension=0, tiled=True
        ).astype(jnp.float32),
    )
    grad_query_rot = grad_query_acc.reshape(token_rows, QUERY_HEADS, HEAD_SIZE) * (
        1.0 / math.sqrt(HEAD_SIZE)
    )
    grad_query_norm = rotary_backward(grad_query_rot, rotary_angles)
    key_norm_gradient = rotary_backward(
        key_gradient_local.reshape(token_rows, KEY_VALUE_HEADS, HEAD_SIZE), rotary_angles
    )
    grad_gain_query = jnp.sum(grad_query_norm * query_rows * inv_query, axis=(0, 1))
    grad_gain_key = jnp.sum(key_norm_gradient * key * key_inverse_norm, axis=(0, 1))
    grad_qk_gain = jnp.concatenate([grad_gain_query, grad_gain_key], axis=0)
    grad_query = (
        norm_backward(query_rows, inv_query, gain_query, grad_query_norm)
        .reshape(token_rows, QUERY_HEADS * HEAD_SIZE)
        .astype(brain_float_half)
    )
    key_gradient = (
        norm_backward(key, key_inverse_norm, key_norm_gain, key_norm_gradient)
        .reshape(token_rows, KEY_VALUE_HEADS * HEAD_SIZE)
        .astype(brain_float_half)
    )
    grad_value = grad_value_own.astype(brain_float_half)
    grad_w_query = jnp.einsum(
        "td,tq->dq", normalized_input, grad_query, preferred_element_type=single_float
    )
    grad_w_key = jnp.einsum(
        "td,tq->dq", normalized_input, key_gradient, preferred_element_type=single_float
    )
    grad_w_value = jnp.einsum(
        "td,tq->dq", normalized_input, grad_value, preferred_element_type=single_float
    )
    grad_normed = jnp.einsum("tq,dq->td", grad_query, query_w, preferred_element_type=single_float)
    grad_normed = grad_normed + jnp.einsum(
        "tq,dq->td", key_gradient, key_matrix, preferred_element_type=single_float
    )
    grad_normed = grad_normed + jnp.einsum(
        "tq,dq->td", grad_value, value_w, preferred_element_type=single_float
    )
    grad_attn_gain = jnp.sum(grad_normed * hidden * inv_one, axis=0)
    grad_in = (grad_middle + norm_backward(hidden, inv_one, gain_one, grad_normed)).astype(
        brain_float_half
    )
    received = (
        lax.all_to_all(
            grad_attn_gain[None].astype(jnp.bfloat16),
            ("ctx", "fsdp"),
            split_axis=1,
            concat_axis=0,
            tiled=True,
        ).astype(jnp.float32),
        lax.all_to_all(
            grad_qk_gain[None].astype(jnp.bfloat16),
            ("ctx", "fsdp"),
            split_axis=1,
            concat_axis=0,
            tiled=True,
        ).astype(jnp.float32),
        lax.all_to_all(
            grad_w_query[None].astype(jnp.bfloat16),
            ("ctx", "fsdp"),
            split_axis=1,
            concat_axis=0,
            tiled=True,
        ).astype(jnp.float32),
        lax.all_to_all(
            grad_w_key[None].astype(jnp.bfloat16),
            ("ctx", "fsdp"),
            split_axis=1,
            concat_axis=0,
            tiled=True,
        ).astype(jnp.float32),
        lax.all_to_all(
            grad_w_value[None].astype(jnp.bfloat16),
            ("ctx", "fsdp"),
            split_axis=1,
            concat_axis=0,
            tiled=True,
        ).astype(jnp.float32),
        lax.all_to_all(
            grad_w_output[None].astype(jnp.bfloat16),
            ("ctx", "fsdp"),
            split_axis=1,
            concat_axis=0,
            tiled=True,
        ).astype(jnp.float32),
        lax.all_to_all(
            grad_ffn_gain[None].astype(jnp.bfloat16),
            ("ctx", "fsdp"),
            split_axis=1,
            concat_axis=0,
            tiled=True,
        ).astype(jnp.float32),
        lax.all_to_all(
            grad_w_gate[None].astype(jnp.bfloat16),
            ("ctx", "fsdp"),
            split_axis=1,
            concat_axis=0,
            tiled=True,
        ).astype(jnp.float32),
        lax.all_to_all(
            grad_w_up[None].astype(jnp.bfloat16),
            ("ctx", "fsdp"),
            split_axis=1,
            concat_axis=0,
            tiled=True,
        ).astype(jnp.float32),
        lax.all_to_all(
            grad_w_down[None].astype(jnp.bfloat16),
            ("ctx", "fsdp"),
            split_axis=1,
            concat_axis=0,
            tiled=True,
        ).astype(jnp.float32),
    )
    summed = owner_totals(received)
    return (
        block_out[None],
        grad_in[None],
        summed[0],
        summed[1],
        summed[2],
        summed[3],
        summed[4],
        summed[5],
        summed[6],
        summed[7],
        summed[8],
        summed[9],
    )


MESH = pl.DeviceIdType.MESH
RANKS = 8
GROUP = QUERY_HEADS // KEY_VALUE_HEADS
COLS = 384
NOTES = 320
PIECES = 4
FIRST_UNITS = 256
VMEM_BYTES = 60 * 1024 * 1024


class Place:
    def __init__(self):
        self.ctx, self.fsdp = lax.axis_index("ctx"), lax.axis_index("fsdp")
        self.half, self.chip = self.ctx // 4, self.ctx % 4
        self.y, self.core = self.fsdp // 2, self.fsdp % 2
        self.rank = self.core * 4 + self.chip
        self.mate = (self.ctx, self.y * 2 + 1 - self.core)
        self.y_peer = (self.ctx, (1 - self.y) * 2 + self.core)
        self.z_peer = ((1 - self.half) * 4 + self.chip, self.fsdp)
        self.swap_peer = ((1 - self.half) * 4 + self.chip, self.y * 2 + 1 - self.core)
        self.stays = self.core == self.half
        self.moves = self.core != self.half

    def chip_at(self, turn):
        low, high = self.chip % 2, self.chip // 2
        low = 1 - low if turn % 2 else low
        high = 1 - high if turn // 2 else high
        return high * 2 + low

    def beside(self, turn):
        low, high = self.chip % 2, self.chip // 2
        low = low + turn % 2 * (1 - 2 * low)
        high = high + turn // 2 * (1 - 2 * high)
        chip = high * 2 + low
        return [self.core * 4 + chip, (1 - self.core) * 4 + chip]

    def member(self, turn, other):
        chip = self.chip_at(turn)
        core = 1 - self.core if other else self.core
        return (self.half * 4 + chip, self.y * 2 + core), chip, core

    def members(self):
        return [self.member(turn, other) for turn in range(4) for other in range(2) if turn or other]

    def ranks(self, turn):
        chip = self.chip_at(turn)
        return self.core * 4 + chip, (1 - self.core) * 4 + chip


class Links:
    def __init__(self, send, receive):
        self.send, self.receive, self.used = send, receive, 0

    def link(self, source, target, device):
        at = self.used
        self.used += 1
        assert at < self.send.shape[0], "semaphores"
        return pltpu.make_async_remote_copy(
            src_ref=source,
            dst_ref=target,
            send_sem=self.send.at[at],
            recv_sem=self.receive.at[at],
            device_id=device,
            device_id_type=MESH,
        )


def greet(devices):
    barrier = pltpu.get_barrier_semaphore()
    for device in devices:
        pl.semaphore_signal(barrier, inc=1, device_id=device, device_id_type=MESH)
    pl.semaphore_wait(barrier, len(devices))


class Spread:
    def __init__(self, place, links, rows, block, by_x=PIECES):
        size = rows.shape[1] // PIECES

        def piece(rank, at):
            return rows.at[rank, pl.ds(at * size, size)]

        own = place.rank
        x_rank, z_rank, far_rank = (place.ranks(turn)[0] for turn in (1, 2, 3))
        x_device, z_device = place.member(1, 0)[0], place.member(2, 0)[0]
        self.order_z = list(range(PIECES))
        self.order_x = self.order_z[by_x:] + self.order_z[:by_x]
        self.by_x, self.pieces = by_x, []
        for at in range(PIECES):
            source = block.at[pl.ds(at * size, size)]
            last, device = (z_rank, x_device) if at < by_x else (x_rank, z_device)
            self.pieces.append(
                dict(
                    near=links.link(source, piece(own, at), place.mate),
                    x=links.link(source, piece(own, at), x_device),
                    z=links.link(source, piece(own, at), z_device),
                    on=links.link(piece(last, at), piece(last, at), device),
                    x_mate=links.link(piece(x_rank, at), piece(x_rank, at), place.mate),
                    z_mate=links.link(piece(z_rank, at), piece(z_rank, at), place.mate),
                    far_mate=links.link(piece(far_rank, at), piece(far_rank, at), place.mate),
                )
            )

    def start(self):
        for at_z, at_x in zip(self.order_z, self.order_x):
            self.pieces[at_z]["z"].start()
            self.pieces[at_x]["x"].start()
        for piece in self.pieces:
            piece["near"].start()

    def start_piece(self, at):
        for name in ("z", "x", "near"):
            self.pieces[at][name].start()

    def relay(self, steps=range(PIECES)):
        for step in steps:
            at_z, at_x = self.order_z[step], self.order_x[step]
            self.pieces[at_z]["z"].wait_recv()
            if at_z < self.by_x:
                self.pieces[at_z]["on"].start()
            self.pieces[at_z]["z_mate"].start()
            self.pieces[at_x]["x"].wait_recv()
            if at_x >= self.by_x:
                self.pieces[at_x]["on"].start()
            self.pieces[at_x]["x_mate"].start()

    def relay_far(self):
        for piece in self.pieces:
            piece["on"].wait_recv()
            piece["far_mate"].start()

    def arrive(self, names=("near", "x_mate", "z_mate", "far_mate")):
        for piece in self.pieces:
            for name in names:
                piece[name].wait_recv()

    def finish(self):
        for piece in self.pieces:
            for copy in piece.values():
                copy.wait_send()


class Collect:
    def __init__(self, place, links, part, near, out, into, out_last, into_last):
        self.place, self.part, self.near = place, part, near
        self.out, self.into, self.out_last, self.into_last = out, into, out_last, into_last
        self.size = part.shape[1] // PIECES
        x_device, z_device = place.member(1, 0)[0], place.member(2, 0)[0]
        self.near_links, self.first, self.last, self.near_done = {}, [], [], False
        for turn in (3, 1, 2, 0):
            other = place.ranks(turn)[1]
            self.near_links[turn] = links.link(part.at[other], near.at[turn], place.mate)
        for at in range(PIECES):
            block, here = self.two_pieces(at)
            self.first.append(links.link(out.at[block, here], into.at[block, here], x_device))
            here = self.rows(at)
            self.last.append(links.link(out_last.at[here], into_last.at[here], z_device))

    def two_pieces(self, at, which=None):
        start = at % 2 * 2 * self.size
        if which is None:
            return at // 2, pl.ds(start, 2 * self.size)
        return at // 2, pl.ds(start + which * self.size, self.size)

    def finish_near(self):
        self.near_done = True
        for copy in self.near_links.values():
            copy.wait_send()

    def send_near(self, turn):
        self.near_links[turn].start()

    def begin(self, turns=(3, 1, 2, 0)):
        for turn in turns:
            self.send_near(turn)

    def rows(self, at):
        return pl.ds(at * self.size, self.size)

    def sum_of(self, turn, at):
        mine = self.part[self.place.ranks(turn)[0], self.rows(at)].astype(jnp.float32)
        return mine + self.near[turn, self.rows(at)].astype(jnp.float32)

    def first_step(self):
        for turn in (3, 1):
            self.near_links[turn].wait_recv()
        for at in range(PIECES):
            for which, turn in enumerate((1, 3)):
                self.out[self.two_pieces(at, which)] = self.sum_of(turn, at).astype(jnp.bfloat16)
            self.first[at].start()

    def second_step(self, sums):
        for turn in (2, 0):
            self.near_links[turn].wait_recv()
        for at in range(PIECES):
            self.first[at].wait_recv()
            total = self.sum_of(2, at) + self.into[self.two_pieces(at, 1)].astype(jnp.float32)
            self.out_last[self.rows(at)] = total.astype(jnp.bfloat16)
            self.last[at].start()
            total = self.sum_of(0, at) + self.into[self.two_pieces(at, 0)].astype(jnp.float32)
            sums[self.rows(at)] = total

    def third_step(self, sums, then=None):
        for at in range(PIECES):
            self.last[at].wait_recv()
            sums[self.rows(at)] += self.into_last[self.rows(at)].astype(jnp.float32)
            if then is not None:
                then(at, self.rows(at))

    def finish(self):
        if not self.near_done:
            self.finish_near()
        for first, last in zip(self.first, self.last):
            first.wait_send()
            last.wait_send()


def collect_scratch(rows, width):
    return [pltpu.VMEM(count + (rows, width), jnp.bfloat16) for count in ((4,), (2,), (2,), (), ())]


COLLECT_LINKS = 4 + 2 * PIECES
SPREAD_LINKS = 7 * PIECES


class Columns:
    def __init__(self, place, links, pieces, whole, local, parts):
        own = whole.at[place.half, place.chip, place.y, place.core]
        self.own = pltpu.make_async_copy(pieces.at[place.chip, place.core], own, local)
        self.square = [
            links.link(pieces.at[chip, core], own, device)
            for device, chip, core in place.members()
        ]
        self.z, self.y, self.y_second = [], [], []
        for lanes in parts:
            here = whole.at[place.half, :, place.y, :, :, lanes]
            there = whole.at[1 - place.half, :, place.y, :, :, lanes]
            self.z.append(links.link(here, here, place.z_peer))
            self.y.append(links.link(here, here, place.y_peer))
            self.y_second.append(links.link(there, there, place.y_peer))

    def start(self):
        self.own.start()
        for copy in self.square:
            copy.start()

    def square_done(self):
        self.own.wait()
        for copy in self.square:
            copy.wait_recv()

    def across(self, part=0):
        self.z[part].start()
        self.y[part].start()

    def relay(self, part=0):
        self.z[part].wait_recv()
        self.y_second[part].start()

    def arrive(self, part=0):
        self.y[part].wait_recv()
        self.y_second[part].wait_recv()

    def finish(self, part=0):
        for copy in (self.z[part], self.y[part], self.y_second[part]):
            copy.wait_send()
        if part == 0:
            for copy in self.square:
                copy.wait_send()


class Rows:
    def __init__(self, place, links, block, whole, local):
        own, pair = whole.at[place.y, place.core], whole.at[place.y]
        self.place = place
        self.own = pltpu.make_async_copy(block, own, local)
        self.mate = links.link(block, own, place.mate)
        self.z = links.link(pair, pair, place.z_peer)
        self.y = links.link(pair, pair, place.y_peer)

    def start(self):
        pl.when(self.place.stays)(self.own.start)
        pl.when(self.place.moves)(self.mate.start)

    def pair_done(self):
        @pl.when(self.place.stays)
        def _():
            self.own.wait()
            self.mate.wait_recv()
            self.z.start()
            self.y.start()

    def relay(self):
        @pl.when(self.place.moves)
        def _():
            self.z.wait_recv()
            self.y.start()

    def arrive(self):
        self.y.wait_recv()

    def finish(self):
        pl.when(self.place.stays)(self.z.wait_send)
        pl.when(self.place.moves)(self.mate.wait_send)
        self.y.wait_send()


def iota(dims, axis):
    return lax.broadcasted_iota(jnp.int32, dims, axis)


def chosen(condition):
    return jnp.where(condition, 1.0, 0.0).astype(jnp.bfloat16)


def dot(a, b):
    return jnp.dot(a, b, preferred_element_type=jnp.float32)


def dot_turned(a, b):
    return lax.dot_general(a, b, (((1,), (1,)), ((), ())), preferred_element_type=jnp.float32)


def dot_fine(a, b):
    high = a.astype(jnp.bfloat16)
    rest = (a - high.astype(jnp.float32)).astype(jnp.bfloat16)
    return dot(high, b) + dot(rest, b)


def dot_fine_turned(b, a):
    high = a.astype(jnp.bfloat16)
    rest = (a - high.astype(jnp.float32)).astype(jnp.bfloat16)
    return dot_turned(b, high) + dot_turned(b, rest)


def head_ones():
    return chosen(iota((256, 256), 0) // HEAD_SIZE == iota((256, 256), 1) // HEAD_SIZE)


def dot_rows(a, b):
    return lax.dot_general(a, b, (((0,), (0,)), ((), ())), preferred_element_type=jnp.float32)


def laid_out(values, row):
    count = values.shape[1]
    table = chosen(iota((count, 128), 1) - (NOTES - 256) == iota((count, 128), 0))
    spread_out = dot(jnp.broadcast_to(values, (16, count)), table)
    return jnp.where(iota((16, 128), 0) == row, spread_out, 0.0)


def gain_rows(notes, width, rows):
    blocks = notes.shape[0] // 16

    def spread_out(at, columns, each):
        lane = iota((128, 1), 0) - (NOTES - 256)
        table = dot(notes[pl.ds(at, blocks, 16)].astype(jnp.bfloat16), chosen(lane == columns % each))
        return jnp.sum(
            jnp.where(iota((blocks, 1), 0) == columns // each, table, 0.0), axis=0, keepdims=True
        )

    column = iota((1, width), 1)
    heads = iota((1, COLS), 1)
    heads = heads % HEAD_SIZE + jnp.where(heads >= GROUP * HEAD_SIZE, HEAD_SIZE, 0)
    return spread_out(0, column, rows), spread_out(1, column, rows), spread_out(2, heads, 4)


class ColumnSums:
    def __init__(self, place, links, whole, final, y_part, far, z_part, local, parts):
        total = y_part.at[0]
        self.place, self.whole, self.y_part = place, whole, y_part
        self.far, self.z_part, self.total = far, z_part, total
        self.y, self.z, self.parts = [], [], parts
        for lanes in parts:
            source = whole.at[1 - place.half, :, 1 - place.y, :, :, lanes]
            self.y.append(links.link(source, y_part.at[0, :, :, :, lanes], place.y_peer))
            every = (slice(None), slice(None), slice(None), lanes)
            self.z.append(links.link(far.at[every], z_part.at[every], place.z_peer))
        source = whole.at[place.half, :, 1 - place.y]
        self.y_near = links.link(source, y_part.at[1], place.y_peer)
        self.own = pltpu.make_async_copy(
            total.at[place.chip, place.core], final.at[place.rank], local
        )
        self.square = [
            links.link(total.at[chip, core], final.at[place.rank], device)
            for device, chip, core in place.members()
        ]

    def start(self, part=0):
        self.y[part].start()

    def start_near(self):
        self.y_near.start()

    def across(self, part=0):
        self.y[part].wait_recv()
        place, lanes = self.place, self.parts[part]

        @pl.loop(0, 4)
        def _(chip):
            mine = self.whole[1 - place.half, chip, place.y, :, :, lanes].astype(jnp.float32)
            both = mine + self.y_part[0, chip, :, :, lanes].astype(jnp.float32)
            self.far[chip, :, :, lanes] = both.astype(jnp.bfloat16)

        self.z[part].start()

    def deal(self):
        self.y_near.wait_recv()
        for copy in self.z:
            copy.wait_recv()
        place = self.place

        @pl.loop(0, 4)
        def _(chip):
            both = self.whole[place.half, chip, place.y].astype(jnp.float32) + self.y_part[
                1, chip
            ].astype(jnp.float32)
            both = both + self.z_part[chip].astype(jnp.float32)
            self.total[chip] = both.astype(jnp.bfloat16)

        self.own.start()
        for copy in self.square:
            copy.start()

    def finish(self):
        self.own.wait()
        for copy in self.square:
            copy.wait()
        for copy in self.y + self.z + [self.y_near]:
            copy.wait_send()


class RowSums:
    def __init__(self, place, links, whole, final, y_part, pair, total):
        z_part, last = pair, total
        self.place, self.whole, self.final, self.y_part = place, whole, final, y_part
        self.pair, self.z_part, self.total, self.last = pair, z_part, total, last
        self.y = links.link(whole.at[1 - place.y], y_part, place.y_peer)
        self.z = links.link(pair, z_part, place.z_peer)
        self.mate = links.link(total, last, place.mate)

    def start(self):
        self.y.start()

    def sum_of(self, core):
        mine = self.whole[self.place.y, core].astype(jnp.float32)
        return mine + self.y_part[core].astype(jnp.float32)

    def across(self):
        self.y.wait_recv()

        @pl.when(self.place.moves)
        def _():
            for core in range(2):
                self.pair[core] = self.sum_of(core).astype(jnp.bfloat16)
            self.z.start()

    def deal(self):
        @pl.when(self.place.stays)
        def _():
            self.z.wait_recv()
            own, other = self.place.core, 1 - self.place.core
            both = self.sum_of(other) + self.z_part[other].astype(jnp.float32)
            self.total[...] = both.astype(jnp.bfloat16)
            self.mate.start()
            self.final[...] = self.sum_of(own) + self.z_part[own].astype(jnp.float32)

    def finish(self):
        self.y.wait_send()

        @pl.when(self.place.stays)
        def _():
            self.mate.wait_send()

        @pl.when(self.place.moves)
        def _():
            self.z.wait_send()
            self.mate.wait_recv()
            self.final[...] = self.last[...].astype(jnp.float32)


def column_scratch(block):
    low = jnp.bfloat16
    return [pltpu.VMEM((2, 4, 2) + block, low)] + [pltpu.VMEM((4, 2) + block, low)] * 2


def row_scratch(block):
    low = jnp.bfloat16
    return [pltpu.VMEM((2,) + block, low)] * 2 + [pltpu.VMEM(block, low)]


def norm_back(values, scale, weighted):
    mean = jnp.mean(weighted * values, axis=-1, keepdims=True)
    return scale * weighted - scale * scale * scale * values * mean


def block_kernel(
    query_w, key_w, value_w, gate_w, up_w, attn_gain, qk_gain, ffn_gain, order, positions,
    out_w, down_w, hidden, cotangent,
    block_out, grad_in, query_sum, key_sum, value_sum, gate_sum, up_sum, out_sum, down_sum, attn_gain_sum, ffn_gain_sum, qk_gain_sum,
    rows, normed, two_all, branch_all, cotangent_all, heads_v, gate_up_v, out_v, down_v,
    inner_t, unit_grad, projected, queries, keys, keys_t, values_t, mixed, mixed_t, totals,
    index_row, index_column, tables, gains,
    key_grad, value_grad, down_grad, scores, probs_grad, inner, gain_sums, gain_parts,
    row_sum, grad_middle, middle, own_low, block_low, in_low, rows_own,
    near_a, first_a, into_a, last_a, into_last_a,
    gate_up_y, gate_up_far, gate_up_z, heads_y, heads_far, heads_z,
    down_y, down_pair, down_t, out_y, out_pair, out_t,
    send, receive, local,
):
    place, links = Place(), Links(send, receive)
    single, low = jnp.float32, jnp.bfloat16
    tokens, width = hidden.shape
    span, head = RANKS * tokens, HEAD_SIZE
    rows_of, units = query_w.shape[0], 4 * down_w.shape[0]
    pair_rows = 2 * tokens
    early = FIRST_UNITS
    late = units // 128 * 128 - early
    unit_parts = [pl.ds(0, 2 * early), pl.ds(2 * early, 2 * (units - early))]
    set_a = (near_a, first_a, into_a, last_a, into_last_a)
    heads_grad = unit_grad.at[:, 0:COLS]
    part, query_grad = rows, mixed
    probs, scores_grad = unit_grad.at[:, COLS : COLS + 256], unit_grad.at[:, COLS + 256 : COLS + 512]

    def moved(source, target, at):
        keep = pltpu.make_async_copy(source, target, local.at[at])
        return keep, links.link(source, target, place.swap_peer)

    def go(pair):
        pl.when(place.stays)(pair[0].start)
        pl.when(place.moves)(pair[1].start)

    def come(pair):
        pl.when(place.stays)(pair[0].wait)
        pl.when(place.moves)(pair[1].wait)

    heads_w, gate_up_w = heads_far, gate_up_far
    notes = key_grad.at[0, 0 : 4 * RANKS * 16]
    landing = cotangent_all.at[4:8].reshape(RANKS, tokens // 2, width)
    heads_sum = landing.at[:, 0:rows_of, 2 * units :]
    gate_up_sum = landing.at[:, 0:rows_of, 0 : 2 * units]
    hidden_move = moved(hidden, rows.at[place.ctx], 0)
    cotangent_move = moved(cotangent, cotangent_all.at[place.ctx], 1)
    block_move = moved(block_low, block_out, 2)
    in_move = moved(in_low, grad_in, 3)
    heads = Columns(place, links, heads_w, heads_v, local.at[4], [pl.ds(0, COLS)])
    out = Rows(place, links, out_w, out_v, local.at[5])
    gate_up = Columns(place, links, gate_up_w, gate_up_v, local.at[6], unit_parts)
    down = Rows(place, links, down_w, down_v, local.at[7])
    hidden_spread = Spread(place, links, rows, rows.at[place.rank])
    cotangent_spread = Spread(place, links, cotangent_all, cotangent_all.at[place.rank])
    two_spread = Spread(place, links, two_all, own_low)
    branch_spread = Spread(place, links, branch_all, own_low)
    attention_collect = Collect(place, links, part, *set_a)
    two_collect = Collect(place, links, part, *set_a)
    down_collect = Collect(
        place, links, part, two_all.at[0:4], two_all.at[4:6], two_all.at[6:8],
        cotangent_all.at[0], cotangent_all.at[1],
    )
    last_collect = Collect(place, links, part, *set_a)
    gate_up_sums = ColumnSums(
        place, links, gate_up_v, gate_up_sum, gate_up_y, gate_up_far, gate_up_z, local.at[8],
        unit_parts,
    )
    heads_sums = ColumnSums(
        place, links, heads_v, heads_sum, heads_y, heads_far, heads_z, local.at[9],
        [pl.ds(0, COLS)],
    )
    down_sums = RowSums(place, links, down_grad, down_sum, down_y, down_pair, down_t)
    out_sums = RowSums(place, links, out_v, out_sum, out_y, out_pair, out_t)

    greet(
        [device for device, _, _ in place.members()]
        + [place.y_peer, place.z_peer, place.swap_peer]
    )
    go(hidden_move)
    out.start()
    down.start()
    first_slot = jnp.sum(
        jnp.where(iota(order.shape, 1) == 2 * place.ctx, order[...].astype(single), 0.0),
        axis=1,
        keepdims=True,
    )
    start = positions[:, 0:1].astype(single) - 64.0 * first_slot
    start_high = jnp.floor(start * (1.0 / 64.0))
    note = laid_out(attn_gain[...], 0) + laid_out(ffn_gain[...], 1) + laid_out(qk_gain[...], 2)
    note = note + laid_out(order[...].astype(single).astype(low), 3)
    at_row, at_lane = iota((16, 128), 0), iota((16, 128), 1) - (NOTES - 256)
    note = note + jnp.where((at_row == 4) & (at_lane == 0), start_high, 0.0)
    note = note + jnp.where((at_row == 4) & (at_lane == 1), start - 64.0 * start_high, 0.0)
    note = jnp.concatenate([note, jnp.zeros((rows_of - 16, 128), single)], axis=0)
    low_part = iota((rows_of, 128), 1) < head
    for rank in range(RANKS):
        odd = rank % 2
        base = rank * GROUP * head - odd * head
        values = query_w[:, base : base + 256].astype(single)
        values = pltpu.roll(values, 256 - head, 1) if odd else values
        base = rank // 2 * 128
        key, value = key_w[:, base : base + 128].astype(single), value_w[:, base : base + 128].astype(single)
        key = key if odd else pltpu.roll(key, head, 1)
        value = pltpu.roll(value, head, 1) if odd else value
        piece = heads_w.at[rank % 4, rank // 4]
        piece[:, 0:128] = values[:, 0:128].astype(low)
        piece[:, 128:256] = jnp.where(low_part, values[:, 128:256], key).astype(low)
        piece[:, 256:COLS] = jnp.where(low_part, value, note).astype(low)
    heads.start()
    for rank in range(RANKS):
        odd = rank % 2
        base = rank * units - odd * head
        wide = units + head
        both_w = []
        for source in (gate_w, up_w):
            values = source[:, base : base + wide].astype(single)
            both_w.append(pltpu.roll(values, wide - head, 1) if odd else values)
        piece, end = gate_up_w.at[rank % 4, rank // 4], early + late
        for side, values in enumerate(both_w):
            piece[:, side * early : (side + 1) * early] = values[:, 0:early].astype(low)
            base = 2 * early + side * (late + 128)
            piece[:, base : base + late] = values[:, early:end].astype(low)
        shared = jnp.where(low_part, both_w[0][:, end:], pltpu.roll(both_w[1][:, end:], head, 1))
        piece[:, 2 * early + late : 2 * early + late + 128] = shared.astype(low)
    gate_up.start()
    out_v[2] = jnp.zeros(out_v.shape[1:], low)
    totals[...] = jnp.zeros(totals.shape, single)
    come(hidden_move)
    hidden_spread.start()
    rows_own[...] = rows[place.rank]
    heads.square_done()
    heads.across()
    go(cotangent_move)

    note = heads_v[place.half, place.chip, place.y, place.half, 0:16, 256:COLS]
    lane = iota((128, span), 0) - (NOTES - 256)
    spread_out = dot(note, chosen(lane == iota((128, span), 1) // 64))
    order_row = jnp.sum(jnp.where(iota((16, span), 0) == 3, spread_out, 0.0), axis=0, keepdims=True)
    row = order_row * 64.0 + (iota((1, span), 1) % 64).astype(single)
    index_row[...] = jnp.broadcast_to(row, (8, span))
    lane = iota((span, 128), 1) - (NOTES - 256)
    spread_out = dot_turned(chosen(lane == iota((span, 128), 0) // 64), note)
    order_column = jnp.sum(
        jnp.where(iota((span, 16), 1) == 3, spread_out, 0.0), axis=1, keepdims=True
    )
    column = order_column * 64.0 + (iota((span, 1), 0) % 64).astype(single)
    index_column[...] = jnp.broadcast_to(column, (span, 128))
    at_row, at_lane = iota((16, 128), 0), iota((16, 128), 1) - (NOTES - 256)
    weight = jnp.where(at_lane == 0, 64.0, 1.0)
    picked = jnp.where((at_row == 4) & (at_lane >= 0) & (at_lane < 2), note.astype(single), 0.0)
    start = jnp.sum(jnp.sum(picked * weight, axis=1, keepdims=True), axis=0, keepdims=True)
    slots = dot_turned(chosen(at_lane == at_row), note)
    first = jnp.sum(jnp.where(iota((16, 16), 1) == 3, slots, 0.0), axis=1, keepdims=True)
    frequency = (iota((8, 128), 1) % (head // 2)).astype(single) * (-2.0 * math.log(THETA) / head)
    frequency = jnp.exp(frequency)[0:1]
    first = (first * 64.0 + start) * frequency
    second = iota((64, 128), 0).astype(single) * frequency
    tables[0:16], tables[16:32] = jnp.cos(first), jnp.sin(first)
    tables[32:96], tables[96:160] = jnp.cos(second), jnp.sin(second)

    def rotation(at):
        cos_b, sin_b = tables[32:96], tables[96:160]
        first_half = (iota((64, 128), 1) % head) < head // 2
        sin_signed = jnp.where(first_half, -sin_b, sin_b)
        cos_signed = jnp.where(first_half, -cos_b, cos_b)
        cosines, sines = [], []
        for slot in range(pair_rows // 64):
            cos_a = tables[pl.ds(at * (pair_rows // 64) + slot, 1)]
            sin_a = tables[pl.ds(16 + at * (pair_rows // 64) + slot, 1)]
            cosines.append(cos_a * cos_b - sin_a * sin_b)
            sines.append(sin_a * cos_signed + cos_a * sin_signed)
        cosine, sine = jnp.concatenate(cosines, axis=0), jnp.concatenate(sines, axis=0)
        return jnp.concatenate([cosine] * 2, axis=1), jnp.concatenate([sine] * 2, axis=1)

    hidden_spread.relay()
    heads.relay()
    out.pair_done()
    gate_up.square_done()
    hidden_spread.relay_far()
    gate_up.across(0)
    hidden_spread.arrive()
    heads.arrive()

    notes[...] = heads_v[:, :, :, :, 0:16, 256:COLS].reshape(notes.shape).astype(single)
    one, second, head_gain = gain_rows(notes, width, rows_of)
    gains[0:1] = one
    gains[1:2] = second
    gains[2:3, 0:COLS] = head_gain
    ones = head_ones()
    first_half = iota((pair_rows, 256), 1) % head < head // 2
    low_lanes = iota((pair_rows, 128), 1) < head

    def pair(at):
        return pl.ds(pl.multiple_of(at * pair_rows, pair_rows), pair_rows)

    def swapped(values):
        return jnp.where(
            first_half, pltpu.roll(values, 256 - head // 2, 1), pltpu.roll(values, head // 2, 1)
        )

    @pl.loop(0, RANKS // 2)
    def _(at):
        here = pair(at)
        for side in range(2):
            for step in range(0, tokens, 32):
                row = rows[at * 2 + side, step : step + 32].astype(single)
                scale = lax.rsqrt(jnp.mean(row * row, axis=-1, keepdims=True) + EPS)
                normed[at * 2 + side, step : step + 32] = (row * scale * gains[0:1]).astype(low)
        flat = normed[pl.ds(at * 2, 2)].reshape(pair_rows, width)
        everything = dot(flat, heads_v[...].reshape(width, COLS))
        raw = everything[:, 0:256]
        projected[here] = raw
        scale = lax.rsqrt(dot_fine(raw * raw, ones) * (1.0 / head) + EPS)
        u = raw * scale * gains[2:3, 0:256]
        cosine, sine = rotation(at)
        turned = u * cosine + swapped(u) * sine
        last = turned[:, 128:256]
        queries[here, 0:128] = (turned[:, 0:128] * 0.125).astype(low)
        queries[here, 128:256] = jnp.where(low_lanes, last * 0.125, 0.0).astype(low)
        key = jnp.where(low_lanes, pltpu.roll(last, head, 1), 0.0)
        value = jnp.where(low_lanes, everything[:, 256:COLS], 0.0)
        both = (key, pltpu.roll(key, head, 1), value, pltpu.roll(value, head, 1))
        for which, each in enumerate(both):
            keys[which, here] = each.astype(low)
        keys_t[0, :, here] = jnp.transpose(key).astype(low)
        keys_t[1, :, here] = jnp.transpose(both[1]).astype(low)
        values_t[0, :, here] = jnp.transpose(value).astype(low)
        values_t[1, :, here] = jnp.transpose(both[3]).astype(low)

    out.relay()
    down.pair_done()
    come(cotangent_move)
    cotangent_spread.start()

    def block(rank):
        return pl.ds(pl.multiple_of(rank * tokens, tokens), tokens)

    def both(ref, ranks, *lanes):
        return jnp.concatenate([ref[(block(rank), *lanes)] for rank in ranks], axis=0)

    def side_by_side(ref, row, ranks):
        return jnp.concatenate([ref[row : row + 1, block(rank)] for rank in ranks], axis=1)

    def half_of(number):
        return slice(number * tokens, (number + 1) * tokens)

    def core_at(at):
        return (1 - place.core) * (1 - at) + place.core * at

    chunk = 128
    chunks = [slice(at, at + chunk) for at in range(0, span, chunk)]

    def grown(here, queries_index):
        keys_index = jnp.concatenate([index_column[here]] * 2, axis=1)
        return jnp.where(keys_index <= queries_index, jnp.exp(scores[here]), 0.0)

    def attend(ranks):
        queries_index = side_by_side(index_row, 0, ranks)
        sums = []
        for number, (which, lanes) in enumerate(((0, 0), (1, 0), (0, 128))):
            scores[...] = dot_turned(keys[which], both(queries, ranks, slice(lanes, lanes + 128)))
            total = jnp.zeros((8, pair_rows), single)
            for here in chunks:
                weight = grown(here, queries_index)
                probs[here] = weight.astype(low)
                total = total + jnp.sum(weight.reshape(chunk // 8, 8, pair_rows), axis=0)
            inverse = 1.0 / jnp.sum(total, axis=0, keepdims=True)
            for side, rank in enumerate(ranks):
                totals[number : number + 1, block(rank)] = inverse[:, half_of(side)]
            sums.append(dot(values_t[which], probs[...]) * inverse)
        first, last = sums[0] + sums[1], sums[2]
        for side, rank in enumerate(ranks):
            here = block(rank)
            mixed_t[0:128, here] = first[:, half_of(side)].astype(low)
            mixed_t[128:256, here] = last[:, half_of(side)].astype(low)
            mixed[here, 0:128] = jnp.transpose(first[:, half_of(side)])
            mixed[here, 128:256] = jnp.transpose(last[:, half_of(side)])

    def in_turns(collect, make, before):
        for turns in ((3, 1), (2, 0)):
            before(turns)
            for turn in turns:
                make(place.ranks(turn)[1])
                collect.send_near(turn)
            for turn in turns:
                make(place.ranks(turn)[0])
            if turns[0] == 3:
                collect.first_step()

    def attend_to(turns):
        chips = [place.chip_at(turn) for turn in turns]

        @pl.loop(0, 2)
        def _(at):
            attend([core_at(at) * 4 + chip for chip in chips])

        if turns[0] == 3:
            cotangent_spread.relay(range(2))
            gate_up.across(1)
            hidden_spread.finish()
            out.arrive()
        else:
            cotangent_spread.relay(range(2, PIECES))

    def branch_part(rank):
        here = block(rank)
        weight = out_v[...].reshape(3 * 2 * rows_of, width)[0:256]
        part[rank] = dot(mixed[here].astype(low), weight).astype(low)

    in_turns(attention_collect, branch_part, attend_to)
    cotangent_spread.relay_far()
    attention_collect.second_step(row_sum)
    gate_up.relay(0)
    down.relay()

    def second_norm(at, rows_here):
        total = rows_own[rows_here].astype(single) + row_sum[rows_here]
        middle[rows_here] = total
        scale = lax.rsqrt(jnp.mean(total * total, axis=-1, keepdims=True) + EPS)
        own_low[rows_here] = (total * scale * gains[1:2]).astype(low)
        two_spread.start_piece(at)

    attention_collect.third_step(row_sum, second_norm)
    two_all[place.rank] = own_low[...]
    attention_collect.finish()
    cotangent_spread.arrive()
    gate_up.arrive(0)
    down.arrive()

    def feed_forward(ranks, lanes, cut, joined, first_unit, count):
        weight = gate_up_v[:, :, :, :, :, lanes].reshape(width, lanes.size)
        normed_rows = jnp.concatenate([two_all[rank] for rank in ranks], axis=0)
        gate_up_rows = dot(normed_rows, weight)
        grad = jnp.concatenate([cotangent_all[rank] for rank in ranks], axis=0)
        weight_down = down_v[...].reshape(units, width)[first_unit : first_unit + count]
        grad_inner = dot_turned(grad, weight_down)
        for side, rank in enumerate(ranks):
            for step in range(0, tokens, 32):
                here = slice(side * tokens + step, side * tokens + step + 32)
                gate, up = cut(gate_up_rows[here])
                back = grad_inner[here]
                if gate.shape[1] > count:
                    rest = jnp.zeros((32, gate.shape[1] - count), single)
                    back = jnp.concatenate([back, rest], axis=1)
                sigmoid = 1.0 / (1.0 + jnp.exp(-gate))
                active = gate * sigmoid
                inner[step : step + 32, 0 : gate.shape[1]] = active * up
                grad_gate = back * up * sigmoid * (1.0 + gate * (1.0 - sigmoid))
                rows_here = pl.ds(pl.multiple_of(rank * tokens + step, 32), 32)
                unit_grad[rows_here, lanes] = joined(grad_gate, back * active).astype(low)
            kept = pl.ds(first_unit, gate.shape[1])
            inner_t[kept, block(rank)] = jnp.transpose(inner[:, 0 : gate.shape[1]]).astype(low)
        return dot_turned(both(unit_grad, ranks, lanes), weight)

    def feed_first(ranks):
        back = feed_forward(
            ranks,
            unit_parts[0],
            lambda values: (values[:, 0:early], values[:, early:]),
            lambda gate, up: jnp.concatenate([gate, up], axis=1),
            0,
            early,
        )
        for side, rank in enumerate(ranks):
            part[rank] = back[half_of(side)].astype(low)

    def cut_second(values):
        shared = values[:, late : late + 128]
        return values[:, 0 : late + 128], jnp.concatenate(
            [values[:, late + 128 :], pltpu.roll(shared, head, 1)], axis=1
        )

    def join_second(gate, up):
        low_part = iota((gate.shape[0], 128), 1) < head
        shared = jnp.where(low_part, gate[:, late:], pltpu.roll(up[:, late:], head, 1))
        return jnp.concatenate([gate[:, 0:late], shared, up[:, 0:late]], axis=1)

    def feed_second(ranks):
        back = feed_forward(
            ranks, unit_parts[1], cut_second, join_second, early, units - early
        )
        for side, rank in enumerate(ranks):
            part[rank] = (part[rank].astype(single) + back[half_of(side)]).astype(low)

    def units_weight_grad(lanes):
        size = width // 4
        for at in range(4):
            columns = two_all[:, :, at * size : (at + 1) * size].reshape(span, size)
            grad = dot_rows(columns, unit_grad[:, lanes]).astype(low)
            chips = pl.ds(at % 2 * 2, 2)
            gate_up_v[at // 2, chips, :, :, :, lanes] = grad.reshape(
                (2,) + gate_up_v.shape[2:5] + (lanes.size,)
            )

    @pl.loop(0, RANKS // 2)
    def _(at):
        @pl.when(at == 0)
        def _():
            two_spread.arrive(["near"])

        @pl.when(at == 1)
        def _():
            two_spread.relay(range(2, PIECES))
            two_spread.arrive(["x_mate"])

        @pl.when(at == 2)
        def _():
            two_spread.arrive(["z_mate"])

        @pl.when(at == 3)
        def _():
            two_spread.arrive(["far_mate"])

        feed_first(place.beside(at))

        @pl.when(at == 0)
        def _():
            two_spread.relay(range(2))

        @pl.when(at == 1)
        def _():
            two_spread.relay_far()
            gate_up.relay(1)


    gate_up.finish(0)
    units_weight_grad(unit_parts[0])
    gate_up_sums.start(0)
    gate_up.arrive(1)

    for turns in ((3, 1), (2, 0)):
        chips = [place.chip_at(turn) for turn in turns]

        @pl.loop(0, 2)
        def _(at):
            feed_second([core_at(at) * 4 + chip for chip in chips])

            @pl.when(at == 0)
            def _():
                two_collect.begin(turns)

        if turns[0] == 3:
            two_collect.first_step()

    gate_up_sums.across(0)
    gate_up.finish(1)
    down.finish()
    units_weight_grad(unit_parts[1])
    gate_up_sums.start(1)
    two_collect.second_step(row_sum)
    size = width // 3
    for at in range(3):
        lanes = slice(at * size, (at + 1) * size)
        columns = cotangent_all[:, :, lanes].reshape(span, size)
        grad = dot(inner_t[0:units], columns).astype(low)
        down_grad[:, :, :, lanes] = grad.reshape(down_grad.shape[:3] + (size,))
    down_sums.start()
    gain_sums[...] = jnp.zeros(gain_sums.shape, single)
    two_spread.finish()
    cotangent_spread.finish()

    def second_norm_back(at, rows_here):
        mid = middle[rows_here]
        scale = lax.rsqrt(jnp.mean(mid * mid, axis=-1, keepdims=True) + EPS)
        grads = row_sum[rows_here]
        gain_sums[1:2] += jnp.sum(grads * mid * scale, axis=0, keepdims=True)
        own_grad = cotangent_all[place.rank, rows_here].astype(single)
        total = own_grad + norm_back(mid, scale, grads * gains[1:2])
        grad_middle[rows_here] = total
        own_low[rows_here] = total.astype(low)
        branch_spread.start_piece(at)

    two_collect.third_step(row_sum, second_norm_back)
    branch_all[place.rank] = own_low[...]
    two_collect.finish()
    key_grad[...] = jnp.zeros(key_grad.shape, single)
    value_grad[...] = jnp.zeros(value_grad.shape, single)
    pick = chosen(iota((8, 256), 1) // head == iota((8, 256), 0))

    def attend_back(at, between):
        ranks = place.beside(at)
        weight = out_v[...].reshape(3 * 2 * rows_of, width)[0:256]
        rows_here = jnp.concatenate([branch_all[rank] for rank in ranks], axis=0)
        all_grad = dot_turned(rows_here, weight)
        product = all_grad.astype(low).astype(single) * both(mixed, ranks, slice(0, 256))
        inverse = jnp.concatenate([totals[:, block(rank)] for rank in ranks], axis=1)
        all_delta = dot_fine_turned(pick, product) * inverse
        high = inverse.astype(low)
        rest = (inverse - high.astype(single)).astype(low)
        all_grad = (all_grad * (dot_rows(high, pick) + dot_rows(rest, pick))).astype(low)
        queries_index = side_by_side(index_row, 0, ranks)
        turned = []
        for number, (which, lanes) in enumerate(((0, 0), (1, 0), (0, 128))):
            query = both(queries, ranks, slice(lanes, lanes + 128))
            grad = all_grad[:, lanes : lanes + 128]
            scores[...] = dot_turned(keys[which], query)
            probs_grad[...] = dot_turned(keys[2 + which], grad)
            for here in chunks:
                weight = grown(here, queries_index)
                probs[here] = weight.astype(low)
                change = weight * (probs_grad[here] - all_delta[number : number + 1])
                scores_grad[here] = change.astype(low)
            value_grad[which] += dot(probs[...], grad)
            key_grad[which] += dot(scores_grad[...], query)
            turned.append(dot(keys_t[which], scores_grad[...]))
            between(number)
        first, last = turned[0] + turned[1], turned[2]
        for side, rank in enumerate(ranks):
            here = block(rank)
            query_grad[here, 0:128] = jnp.transpose(first[:, half_of(side)]) * 0.125
            query_grad[here, 128:256] = jnp.transpose(last[:, half_of(side)]) * 0.125

    @pl.loop(0, 2)
    def _(at):
        @pl.when(at == 0)
        def _():
            branch_spread.arrive(["near"])

        @pl.when(at == 1)
        def _():
            branch_spread.arrive(["x_mate"])

        def between(number):
            @pl.when(at == 0)
            def _():
                branch_spread.relay(((0, 1), (2,), (3,))[number])

            if number == 0:
                pl.when(at == 1)(branch_spread.relay_far)
                pl.when(at == 1)(lambda: gate_up_sums.across(1))

        attend_back(at, between)


    @pl.loop(0, RANKS // 2)
    def _(at):
        here = pair(at)
        rows_part = dot_rows(inner_t[0:units, here], down_v[...].reshape(units, width))
        part[pl.ds(at * 2, 2)] = rows_part.astype(low).reshape(2, tokens, width)

    down_collect.begin()
    gate_up_sums.start_near()

    @pl.loop(2, RANKS // 2)
    def _(at):
        @pl.when(at == 2)
        def _():
            branch_spread.arrive(["z_mate"])

        @pl.when(at == 3)
        def _():
            branch_spread.arrive(["far_mate"])

        def between(number):
            if number == 0:
                pl.when(at == 2)(down_collect.first_step)
                pl.when(at == 3)(down_sums.across)

        attend_back(at, between)

    out.finish()
    flat = branch_all[...].reshape(span, width)
    out_v[0:2] = dot(mixed_t[0 : GROUP * head], flat).astype(low).reshape((2,) + out_v.shape[1:])
    out_sums.start()

    @pl.loop(0, RANKS // 2)
    def _(at):
        here = pair(at)
        merged = []
        for sums in (key_grad, value_grad):
            total = jnp.where(low_lanes, sums[0, here] + pltpu.roll(sums[1, here], head, 1), 0.0)
            merged.append(total)
        second = query_grad[here, 128:256] + pltpu.roll(merged[0], head, 1)
        grad = jnp.concatenate([query_grad[here, 0:128], second], axis=1)
        cosine, sine = rotation(at)
        turned = grad * cosine - swapped(grad) * sine
        raw = projected[here]
        scale = lax.rsqrt(dot_fine(raw * raw, ones) * (1.0 / head) + EPS)
        gain_sums[2:3, 0:256] += jnp.sum(turned * raw * scale, axis=0, keepdims=True)
        weighted = turned * gains[2:3, 0:256]
        mean = dot_fine(weighted * raw, ones) * (1.0 / head)
        back = scale * weighted - scale * scale * scale * raw * mean
        heads_grad[here, 0:256] = back.astype(low)
        heads_grad[here, 256:COLS] = merged[1].astype(low)

    down_collect.second_step(row_sum)

    def normed_part(rank):
        here = block(rank)
        part[rank] = dot_turned(heads_grad[here], heads_v[...].reshape(width, COLS)).astype(low)

    branch_spread.finish()
    down_collect.finish_near()
    in_turns(last_collect, normed_part, lambda turns: None)
    out_sums.across()
    heads.finish()
    size = width // 4
    for at in range(4):
        columns = normed[:, :, at * size : (at + 1) * size].reshape(span, size)
        grad = dot_rows(columns, heads_grad[...]).astype(low)
        chips = pl.ds(at % 2 * 2, 2)
        heads_v[at // 2, chips] = grad.reshape((2,) + heads_v.shape[2:])
    heads_sums.start()
    heads_sums.start_near()
    down_collect.third_step(row_sum)
    block_low[...] = (middle[...] + row_sum[...]).astype(low)
    go(block_move)
    down_collect.finish()
    last_collect.second_step(row_sum)
    heads_sums.across()

    def first_norm_back(at, rows_here):
        values = rows_own[rows_here].astype(single)
        scale = lax.rsqrt(jnp.mean(values * values, axis=-1, keepdims=True) + EPS)
        grads = row_sum[rows_here]
        gain_sums[0:1] += jnp.sum(grads * values * scale, axis=0, keepdims=True)
        total = grad_middle[rows_here] + norm_back(values, scale, grads * gains[0:1])
        in_low[rows_here] = total.astype(low)

    last_collect.third_step(row_sum, first_norm_back)
    go(in_move)
    exchanges = []
    for at, device in enumerate(
        (place.mate, place.member(1, 0)[0], place.member(2, 0)[0], place.y_peer, place.z_peer)
    ):
        source = gain_sums if at == 0 else gain_parts.at[5 + at]
        exchanges.append(links.link(source, gain_parts.at[at], device))

    def exchange(at):
        exchanges[at].wait_recv()
        source = gain_sums if at == 0 else gain_parts.at[5 + at]
        gain_parts[6 + at] = source[...] + gain_parts[at]
        if at < 4:
            exchanges[at + 1].start()

    exchanges[0].start()
    gate_up_sums.deal()
    exchange(0)
    down_sums.deal()
    exchange(1)
    out_sums.deal()
    exchange(2)
    heads_sums.deal()
    exchange(3)
    for each in (last_collect, down_sums, out_sums):
        each.finish()
    exchange(4)
    total = gain_parts[10]
    block_at = place.ctx * 4 + place.fsdp
    pick_rows = chosen(iota((width, 128), 0) == iota((width, 128), 1) + block_at * rows_of)
    in_block = iota((width, 128), 1) < rows_of
    own = dot_fine(total, jnp.where(in_block, pick_rows, jnp.zeros_like(pick_rows)))
    attn_gain_sum[...] = own[0:1, 0:rows_of]
    ffn_gain_sum[...] = own[1:2, 0:rows_of]
    lanes, columns = iota((256, 128), 0), iota((256, 128), 1)
    gain_at = lanes % head + jnp.where(lanes >= GROUP * head, head, 0)
    own = dot_fine(total[:, 0:256], chosen((gain_at == columns + block_at * 4) & (columns < 4)))
    qk_gain_sum[...] = own[2:3, 0:4]
    for copy in exchanges:
        copy.wait_send()
    gate_up_sums.finish()
    low_part = iota((rows_of, 128), 1) < head

    def joined_up(rank, parts):
        first, second = (parts(rank + side) for side in range(2))
        moved_by = pltpu.roll(second, head, 1)
        count = first.shape[1] - 128
        middle_tile = jnp.where(low_part, first[:, count:], moved_by[:, 0:128])
        return jnp.concatenate([first[:, 0:count], middle_tile, moved_by[:, 128:]], axis=1)

    def gate_part(rank):
        return jnp.concatenate(
            [
                gate_up_sum[rank, :, 0:early],
                gate_up_sum[rank, :, 2 * early : 2 * early + late + 128],
            ],
            axis=1,
        ).astype(single)

    def up_part(rank):
        shared = gate_up_sum[rank, :, 2 * early + late : 2 * early + late + 128].astype(single)
        return jnp.concatenate(
            [
                gate_up_sum[rank, :, early : 2 * early].astype(single),
                gate_up_sum[rank, :, 2 * early + late + 128 :].astype(single),
                pltpu.roll(shared, head, 1),
            ],
            axis=1,
        )

    for rank in range(0, RANKS, 2):
        lanes = slice(rank * units, (rank + 2) * units)
        gate_sum[:, lanes] = joined_up(rank, gate_part)
        up_sum[:, lanes] = joined_up(rank, up_part)
    heads_sums.finish()
    for rank in range(0, RANKS, 2):
        lanes = slice(rank * GROUP * head, (rank + 2) * GROUP * head)
        query_sum[:, lanes] = joined_up(
            rank, lambda at: heads_sum[at, :, 0:256].astype(single)
        )
        lanes = slice(rank * head, (rank + 2) * head)
        first = heads_sum[rank, :, 128:256].astype(single)
        second = heads_sum[rank + 1, :, 128:256].astype(single)
        key_sum[:, lanes] = jnp.where(low_part, pltpu.roll(first, head, 1), second)
        first = heads_sum[rank, :, 256:COLS].astype(single)
        second = heads_sum[rank + 1, :, 256:COLS].astype(single)
        value_sum[:, lanes] = jnp.where(low_part, first, pltpu.roll(second, head, 1))
    come(block_move)
    come(in_move)


ANYWHERE = pl.BlockSpec(memory_space=pl.ANY)
ON_CHIP = pl.BlockSpec(memory_space=pltpu.VMEM)


def call(kernel, name, number, outs, scratch, ins, in_specs, out_specs):
    return pl.pallas_call(
        kernel,
        out_shape=outs,
        in_specs=in_specs,
        out_specs=out_specs,
        scratch_shapes=scratch,
        name=name,
        compiler_params=pltpu.CompilerParams(
            collective_id=number, has_side_effects=True, vmem_limit_bytes=VMEM_BYTES
        ),
    )(*ins)


def shape(dims, kind=jnp.bfloat16):
    return jax.ShapeDtypeStruct(dims, kind)


def copies(count):
    return [pltpu.SemaphoreType.DMA((count,)), pltpu.SemaphoreType.DMA((count,))]
def square_plan(
    hidden_in,
    cotangent,
    block_order,
    rotary_positions,
    attn_gain,
    qk_gain,
    w_query,
    key_projection,
    value_projection,
    w_output,
    ffn_gain,
    w_gate,
    w_up,
    w_down,
):
    single, low = jnp.float32, jnp.bfloat16
    place = Place()
    tokens, width = hidden_in.shape[1:]
    span = RANKS * tokens
    rows = w_query.shape[0]
    ff = w_gate.shape[1] // RANKS
    q_cols, head = GROUP * HEAD_SIZE, HEAD_SIZE
    cols = 384
    half_rows = tokens // 2
    order = block_order[0]

    early, cut = FIRST_UNITS, ff // 128 * 128
    block, many = (tokens, width), (RANKS, tokens, width)

    def held(*dims, kind=low):
        return pltpu.VMEM(dims, kind)

    results = call(
        block_kernel,
        "whole_block",
        0,
        [
            shape(block),
            shape(block),
            shape(w_query.shape, single),
            shape(key_projection.shape, single),
            shape(value_projection.shape, single),
            shape(w_gate.shape, single),
            shape(w_up.shape, single),
            shape(w_output.shape, single),
            shape(w_down.shape, single),
            shape((1, rows), single),
            shape((1, rows), single),
            shape((1, qk_gain.shape[0]), single),
        ],
        [
            held(*many),
            held(*many),
            held(*many),
            held(*many),
            held(*many),
            held(2, 4, 2, 2, rows, cols),
            held(2, 4, 2, 2, rows, 2 * ff),
            held(3, 2, *w_output.shape),
            held(2, 2, *w_down.shape),
            held(cut + 128, span),
            held(span, 2 * ff),
            held(span, 256, kind=single),
            held(span, 256),
            held(4, span, 128),
            held(2, 128, span),
            held(2, 128, span),
            held(span, 256, kind=single),
            held(256, span),
            held(8, span, kind=single),
            held(8, span, kind=single),
            held(span, 128, kind=single),
            held(160, 128, kind=single),
            held(8, width, kind=single),
            held(2, span, 128, kind=single),
            held(2, span, 128, kind=single),
            held(2, 2, *w_down.shape),
            held(span, 256, kind=single),
            held(span, 256, kind=single),
            held(tokens, cut + 128 - early, kind=single),
            held(8, width, kind=single),
            held(11, 8, width, kind=single),
            held(*block, kind=single),
            held(*block, kind=single),
            held(*block, kind=single),
            held(*block),
            held(*block),
            held(*block),
            held(*block),
        ]
        + collect_scratch(tokens, width)
        + column_scratch((rows, 2 * ff))
        + column_scratch((rows, cols))
        + row_scratch(w_down.shape)
        + row_scratch(w_output.shape)
        + copies(4 + 10 + 13 + 6 + 4 * SPREAD_LINKS + 4 * COLLECT_LINKS + 22 + 6 + 5)
        + [pltpu.SemaphoreType.DMA((11,))],
        (
            w_query, key_projection, value_projection, w_gate, w_up,
            attn_gain[None], qk_gain[None], ffn_gain[None], block_order, rotary_positions,
            w_output, w_down, hidden_in[0], cotangent[0],
        ),
        [ON_CHIP] * 10 + [ANYWHERE] * 4,
        [ANYWHERE] * 2 + [ON_CHIP] * 10,
    )
    block_out, grad_in, query_sum, key_sum, value_sum, gate_sum, up_sum, out_sum, down_sum = results[:9]
    attn_gain_sum, ffn_gain_sum, qk_gain_sum = results[9:]
    return (
        block_out[None],
        grad_in[None],
        attn_gain_sum[0],
        qk_gain_sum[0],
        query_sum,
        key_sum,
        value_sum,
        out_sum,
        ffn_gain_sum[0],
        gate_sum,
        up_sum,
        down_sum,
    )


def solution(mesh):
    square = dict(mesh.shape) == {"ctx": 8, "fsdp": 4}
    plan = square_plan if square else general_plan
    return jax.shard_map(
        plan,
        mesh=mesh,
        in_specs=(
            P("fsdp", "ctx", None),
            P("fsdp", "ctx", None),
            P("fsdp", None),
            P("fsdp", "ctx"),
            P(("ctx", "fsdp")),
            P(("ctx", "fsdp")),
            P(("ctx", "fsdp"), None),
            P(("ctx", "fsdp"), None),
            P(("ctx", "fsdp"), None),
            P(("ctx", "fsdp"), None),
            P(("ctx", "fsdp")),
            P(("ctx", "fsdp"), None),
            P(("ctx", "fsdp"), None),
            P(("ctx", "fsdp"), None),
        ),
        out_specs=(
            P("fsdp", "ctx", None),
            P("fsdp", "ctx", None),
            P(("ctx", "fsdp")),
            P(("ctx", "fsdp")),
            P(("ctx", "fsdp"), None),
            P(("ctx", "fsdp"), None),
            P(("ctx", "fsdp"), None),
            P(("ctx", "fsdp"), None),
            P(("ctx", "fsdp")),
            P(("ctx", "fsdp"), None),
            P(("ctx", "fsdp"), None),
            P(("ctx", "fsdp"), None),
        ),
        check_vma=False,
    )
```
